32 devices in a mesh: views: 2 (over x), depth: 2 (over core), lat: 8 (over z, y).
Axes of the slice: x: 2, y: 2, z: 4, core: 2. Of those that a mesh axis runs over, the one named last changes fastest.
Arguments:
- volume: bfloat16 [256, 128, 2048], P(('views', 'depth'), 'lat'), parts along dimension 0, may hold values from -6 to 6
- shift_table: int32 [256], P('views'), parts along dimension 0, may hold values from 0 to 48, as said below
- slab_order: int32 [16, 2], P(('views', 'lat')), parts along dimension 0, may hold values from 0 to 1, each once within a row
- centers: float32 [8], replicated, may hold values from -2 to 2
- widths: float32 [8], replicated, may hold values from 0.5 to 4
- extinct: float32 [8], replicated, may hold values from 0.2 to 3
- colors: float32 [3, 8], replicated, may hold values from 0 to 1
Outputs:
- image: float32 [4, 256, 2048], P(None, ('views', 'lat'), 'depth'), parts along dimension 1
The draws below stay inside these ranges and needn't reach their ends.
There are 2 independent parts, one for each index of `views`. The reference program is written for one: setup_inputs(seed, part) draws one part's arguments, and reference() takes and returns one part's arrays. A program takes and returns all parts, laid end to end along the dimension named above; an argument that names none is the same for every part. Nothing has to cross between parts.
Inputs may be any that keep to these rules, and one draw needn't show every extreme that they name: `shift_table`: every slice's shift lies in 0 to 48; some slice has shift 0 and some slice has shift exactly 48. `slab_order`: each row is a permutation of the slab indices; its entry 0 is the slab nearest the eye for that band of rows.
All inputs are finite; a program needn't handle non-finite values.
Results may differ from the reference program's by a relative error of at most 0.0003.
Values may be sent and summed in bfloat16 or wider, within the bound.
A program may use at most 128 MiB of HBM per device.

```python
import math
import jax
import jax.numpy as jnp
from jax import lax

NX = 2048
ROWS_DEV = 16
LOBES = 8
NY = 128
NZ = 128
N_DEPTH = 2
N_LAT = 8


def draw_shift_table(key, part):
    values = jax.random.randint(key, (NZ,), 0, 3 * ROWS_DEV + 1, dtype=jnp.int32)
    where_high = jax.random.randint(jax.random.fold_in(key, 11), (), 0, NZ, dtype=jnp.int32)
    values = values.at[where_high].set(3 * ROWS_DEV)
    values = values.at[(where_high + 1) % NZ].set(0)
    return values


def block_levels(stream_key, dims, shards, low, top_value):
    gain = 1.0
    for position, parts in shards:
        steps = jax.random.uniform(jax.random.fold_in(jax.random.fold_in(stream_key, 6), position), (parts,), jnp.float32, low / len(shards), top_value / len(shards))
        gain = gain * jnp.repeat(jnp.exp(steps), dims[position] // parts).reshape((-1,) + (1,) * (len(dims) - 1 - position))
    return gain


def centred(stream_key, extent, width, bound, shards=(), kind=jnp.bfloat16):
    values = jax.random.normal(stream_key, extent, jnp.float32) * width
    if len(shards) > 0:
        values = block_levels(stream_key, extent, shards, -0.22, 0.18) * values
    return jnp.clip(values, min=-bound, max=bound).astype(kind)


def setup_inputs(seed: int = 0, part: int = 0) -> dict:
    key_of = jax.random.split(jax.random.key(seed), 8)
    part_splits = jax.random.split(jax.random.fold_in(key_of[7], part), 8)
    return {
        "volume": centred(part_splits[0], (NZ, NY, NX), 1.0, 6.0, ((0, 2), (1, 8))),
        "shift_table": draw_shift_table(jax.random.fold_in(jax.random.fold_in(key_of[7], part), 71), part),
        "slab_order": jax.vmap(lambda own: jax.random.permutation(own, N_DEPTH))(jax.random.split(part_splits[2], N_LAT)).reshape((N_LAT, N_DEPTH)).astype(jnp.int32),
        "centers": jnp.clip(jax.random.uniform(key_of[3], (LOBES,), jnp.float32, -2.0, 2.0), -2.0, 2.0),
        "widths": jnp.clip(jnp.exp(jax.random.uniform(key_of[4], (LOBES,), jnp.float32, math.log(0.5), math.log(4.0))), 0.5, 4.0),
        "extinct": jnp.clip(jnp.exp(jax.random.uniform(key_of[5], (LOBES,), jnp.float32, math.log(0.2), math.log(3.0))), 0.2, 3.0),
        "colors": jnp.clip(jax.random.uniform(key_of[6], (3, LOBES), jnp.float32, 0.0, 1.0), 0.0, 1.0),
    }


def classify(samples, centers, widths, extinct, colors, inv_depth):
    optical = jnp.zeros(samples.shape, jnp.float32)
    emission = jnp.zeros((3,) + samples.shape, jnp.float32)
    for lobe_index in range(centers.shape[0]):
        lobe_value = jnp.exp(-jnp.square(samples - centers[lobe_index]) * widths[lobe_index])
        optical = optical + extinct[lobe_index] * lobe_value
        emission = emission + colors[:, lobe_index].reshape((3,) + (1,) * samples.ndim) * lobe_value[None]
    return optical * inv_depth, emission


def composite(padded, shift_table, centers, widths, extinct, colors, forward, inv_depth):
    slice_count = padded.shape[0]
    row_count = padded.shape[1] - 3 * ROWS_DEV
    col_count = padded.shape[2]

    def advance(running, counter):
        depth_sum, color = running
        if forward:
            slice_index = counter
        else:
            slice_index = (slice_count - 1 - counter).astype(jnp.int32)
        offset = shift_table[slice_index].astype(jnp.int32)
        slice_plane = lax.dynamic_slice(padded, (slice_index, offset, jnp.int32(0)), (1, row_count, col_count))[0]
        optical, emission = classify(slice_plane.astype(jnp.float32), centers, widths, extinct, colors, inv_depth)
        weight = jnp.exp(-depth_sum) * (1.0 - jnp.exp(-optical))
        return (depth_sum + optical, color + weight[None] * emission), None

    start = (jnp.zeros((row_count, col_count), jnp.float32), jnp.zeros((3, row_count, col_count), jnp.float32))
    (depth_sum, color), _ = lax.scan(advance, start, jnp.arange(slice_count, dtype=jnp.int32))
    return depth_sum, color


def reference(volume, shift_table, slab_order, centers, widths, extinct, colors):
    reach = 3 * ROWS_DEV
    padded = jnp.pad(volume, ((0, 0), (0, reach), (0, 0)))
    inv_depth = 1.0 / NZ
    depth_sum, color_front = composite(padded, shift_table, centers, widths, extinct, colors, True, inv_depth)
    depth_back, color_back = composite(padded, shift_table, centers, widths, extinct, colors, False, inv_depth)
    row_forward = jnp.repeat(slab_order[:, 0] == 0, ROWS_DEV)
    color = jnp.where(row_forward[None, :, None], color_front, color_back)
    return jnp.concatenate([color, (1.0 - jnp.exp(-depth_sum))[None]], axis=0)
```

```python
import jax
import jax.numpy as jnp
from jax import lax
from jax.experimental import pallas as pl
from jax.experimental.pallas import tpu as pltpu
from jax.sharding import PartitionSpec as P

CHUNKS = 4
BLOCK = 256
LANES = 128


def from_behind(block, axis, distance):
    devices = range(lax.axis_size(axis))
    route = [(i - distance, i) for i in devices if i - distance in devices]
    return lax.ppermute(block, axis, route)


def max_over(value, axis):
    size = lax.axis_size(axis)
    best = value
    for step in range(1, size):
        route = [(i, (i + step) % size) for i in range(size)]
        best = jnp.maximum(best, lax.ppermute(value, axis, route))
    return best


def exclusive(counts):
    z = jnp.arange(counts.shape[0], dtype=jnp.int32)
    return jnp.sum(jnp.where(z[None, :] < z[:, None], counts[None, :], 0), axis=1)


def positions(wanted):
    slices, rows = wanted.shape
    ones = wanted.astype(jnp.int32)
    base = exclusive(jnp.sum(ones, axis=1))
    r = jnp.arange(rows, dtype=jnp.int32)
    rank = jnp.sum(jnp.where(r[None, :, None] > r[None, None, :], ones[:, None, :], 0), axis=2)
    return jnp.where(wanted, base[:, None] + rank, -1)


def plan(local_shift, rows):
    source = jnp.arange(rows, dtype=jnp.int32)[None, :]
    target = (source - local_shift[:, None]) % rows
    far = (target + local_shift[:, None]) // rows
    return target, far


def one_hot(place, count):
    return (place.reshape(1, -1) == jnp.arange(count, dtype=jnp.int32)[:, None]).astype(jnp.bfloat16)


def render_kernel(slices, rows, front_ref, par_ref, own_m, two_m, odd_m, own, two, odd, out_ref, cells):
    lobes = par_ref.shape[1]
    tile = 256

    @pl.loop(0, cells.shape[0], step=tile)
    def _(start):
        at = pl.ds(pl.multiple_of(start, tile), tile)
        cells[at, :] = (
            jnp.dot(own_m[at, :], own[...], preferred_element_type=jnp.float32)
            + jnp.dot(two_m[at, :], two[...], preferred_element_type=jnp.float32)
            + jnp.dot(odd_m[at, :], odd[...], preferred_element_type=jnp.float32)
        )

    forward = front_ref[0, 0] == 0
    for part in range(out_ref.shape[2] // LANES):
        lanes = slice(part * LANES, (part + 1) * LANES)

        def advance(i, carry):
            depth, clear, red, green, blue = carry
            z = jnp.where(forward, i, slices - 1 - i)
            samples = cells[pl.ds(pl.multiple_of(z * rows, rows), rows), lanes]
            sums = None
            for k in range(lobes):
                off = samples - par_ref[0, k]
                lobe = jnp.exp(off * off * par_ref[1, k])
                terms = [par_ref[2 + j, k] * lobe for j in range(4)]
                sums = terms if sums is None else [a + b for a, b in zip(sums, terms)]
            depth = depth + sums[0]
            after = jnp.exp(-depth)
            weight = clear - after
            return (depth, after, red + weight * sums[1], green + weight * sums[2], blue + weight * sums[3])

        zero = jnp.zeros((rows, LANES), jnp.float32)
        depth, _, red, green, blue = lax.fori_loop(
            0, slices, advance, (zero, zero + 1.0, zero, zero, zero), unroll=2
        )
        out_ref[0, :, lanes] = red
        out_ref[1, :, lanes] = green
        out_ref[2, :, lanes] = blue
        out_ref[3, :, lanes] = depth


def render(front, params, matrices, own, two, odd, slices, rows):
    cols = own.shape[1]
    block = min(BLOCK, cols)

    def whole(m):
        return pl.BlockSpec(m.shape, lambda c: (0, 0))

    def columns(a):
        return pl.BlockSpec((a.shape[0], block), lambda c: (0, c))

    smem = pl.BlockSpec(memory_space=pltpu.SMEM)
    cells = slices * rows * cols
    return pl.pallas_call(
        lambda *refs: render_kernel(slices, rows, *refs),
        out_shape=jax.ShapeDtypeStruct((4, rows, cols), jnp.float32),
        grid=(cols // block,),
        in_specs=[smem, smem] + [whole(m) for m in matrices] + [columns(a) for a in (own, two, odd)],
        out_specs=pl.BlockSpec((4, rows, block), lambda c: (0, 0, c)),
        scratch_shapes=[pltpu.VMEM((slices * rows, block), jnp.float32)],
        compiler_params=pltpu.CompilerParams(vmem_limit_bytes=40 * 1024 * 1024),
        cost_estimate=pl.CostEstimate(flops=cells * 6000, bytes_accessed=cells * 6, transcendentals=cells * 9),
        name="render",
    )(front, params, *matrices, own, two, odd)


def pick(matrix, rows):
    return jnp.dot(matrix, rows, preferred_element_type=jnp.float32).astype(jnp.bfloat16)


def partial_image(two_cap, odd_cap, volume, local_shift, front, params):
    slices, rows, cols = volume.shape
    total = slices * rows
    target, far = plan(local_shift, rows)
    two_at = positions(far >= 2)
    odd_at = positions(far % 2 == 1)
    two_send = one_hot(two_at, two_cap)
    odd_own = one_hot(jnp.where(far == 1, odd_at, -1), odd_cap)
    two_index = jnp.arange(two_cap, dtype=jnp.int32)
    hop = jnp.where(far == 3, two_at, -1).reshape(1, -1)
    odd_two = jnp.dot(
        one_hot(odd_at, odd_cap),
        (hop.reshape(-1, 1) == two_index[None, :]).astype(jnp.bfloat16),
        preferred_element_type=jnp.float32,
    ).astype(jnp.bfloat16)
    source = jnp.arange(rows, dtype=jnp.int32)
    picks = target[:, None, :] == source[None, :, None]

    def by_target(values):
        return jnp.max(jnp.where(picks, values[:, None, :], -1), axis=2).reshape(-1, 1)

    flat = jnp.arange(total, dtype=jnp.int32).reshape(slices, rows)

    def place(values, count):
        return (by_target(values) == jnp.arange(count, dtype=jnp.int32)[None, :]).astype(jnp.bfloat16)

    matrices = (
        place(jnp.where(far == 0, flat, -1), total),
        place(jnp.where(far == 2, two_at, -1), two_cap),
        place(odd_at, odd_cap),
    )
    field = volume.reshape(total, cols)
    width = cols // CHUNKS
    parts = []
    for c in range(CHUNKS):
        own = field[:, c * width : (c + 1) * width]
        two = from_behind(pick(two_send, own), "lat", -2)
        relay = jnp.dot(odd_own, own, preferred_element_type=jnp.float32) + jnp.dot(
            odd_two, two, preferred_element_type=jnp.float32
        )
        odd = from_behind(relay.astype(jnp.bfloat16), "lat", -1)
        parts.append(render(front, params, matrices, own, two, odd, slices, rows))
    return jnp.concatenate(parts, axis=2)


def local(volume, shift_table, slab_order, centers, widths, extinct, colors):
    slabs = lax.axis_size("depth")
    slices, rows, cols = volume.shape
    total = slices * rows
    inv_depth = 1.0 / (slices * slabs)
    params = jnp.concatenate([centers[None], -widths[None], (extinct * inv_depth)[None], colors], axis=0)
    slab = lax.axis_index("depth")
    local_shift = lax.dynamic_slice_in_dim(shift_table, slab * slices, slices)
    two_cap, odd_cap = total * 11 // 16, total * 10 // 16
    over = jnp.zeros((), jnp.int32)
    _, all_far = plan(shift_table, rows)
    for s in range(slabs):
        far = all_far[s * slices : (s + 1) * slices]
        over = jnp.maximum(over, jnp.sum((far >= 2).astype(jnp.int32)) - two_cap)
        over = jnp.maximum(over, jnp.sum((far % 2 == 1).astype(jnp.int32)) - odd_cap)
    over = max_over(over.reshape(1, 1), "views")[0, 0]
    partial_value = lax.cond(
        over > 0,
        lambda *a: partial_image(total, total, *a),
        lambda *a: partial_image(two_cap, odd_cap, *a),
        volume,
        local_shift,
        slab_order,
        params,
    )
    own_cols = cols // slabs
    theirs = lax.dynamic_slice_in_dim(partial_value, (1 - slab) * own_cols, own_cols, 2)
    mine = lax.dynamic_slice_in_dim(partial_value, slab * own_cols, own_cols, 2)
    other = lax.ppermute(theirs, "depth", [(0, 1), (1, 0)])
    mine_first = slab_order[0, 0] == slab
    front = jnp.where(mine_first, mine, other)
    back = jnp.where(mine_first, other, mine)
    color = front[:3] + jnp.exp(-front[3])[None] * back[:3]
    opacity = 1.0 - jnp.exp(-(mine[3] + other[3]))
    return jnp.concatenate([color, opacity[None]], axis=0)


def solution(mesh):
    in_specs = (
        P(("views", "depth"), "lat", None),
        P("views"),
        P(("views", "lat"), None),
        P(),
        P(),
        P(),
        P(),
    )
    out_specs = P(None, ("views", "lat"), "depth")
    return jax.shard_map(local, mesh=mesh, in_specs=in_specs, out_specs=out_specs, check_vma=False)
```

```python
import math
import jax
import jax.numpy as jnp
from jax import lax
from jax.experimental import pallas as pl
from jax.experimental.pallas import tpu as pltpu
from jax.sharding import PartitionSpec as P

CHUNKS = 4
LANES = 128


def along_lat(block, distance):
    devices = range(lax.axis_size("lat"))
    route = [(i, i + distance) for i in devices if i + distance in devices]
    return lax.ppermute(block, "lat", route)


def max_over(value, axis):
    size = lax.axis_size(axis)
    best = value
    for step in range(1, size):
        route = [(i, (i + step) % size) for i in range(size)]
        best = jnp.maximum(best, lax.ppermute(value, axis, route))
    return best


def positions(wanted):
    slices, rows = wanted.shape
    ones = wanted.astype(jnp.int32)
    z = jnp.arange(slices, dtype=jnp.int32)
    counts = jnp.sum(ones, axis=1)
    base = jnp.sum(jnp.where(z[None, :] < z[:, None], counts[None, :], 0), axis=1)
    r = jnp.arange(rows, dtype=jnp.int32)
    rank = jnp.sum(jnp.where(r[None, :, None] > r[None, None, :], ones[:, None, :], 0), axis=2)
    return jnp.where(wanted, base[:, None] + rank, -1)


def plan(shift, rows):
    source = jnp.arange(rows, dtype=jnp.int32)[None, :]
    target = (source - shift[:, None]) % rows
    far = (target + shift[:, None]) // rows
    return target, far


def tables(shift, rows, caps):
    slices = shift.shape[0]
    target, far = plan(shift, rows)
    flat = jnp.arange(slices * rows, dtype=jnp.int32).reshape(slices, rows)
    r = jnp.arange(rows, dtype=jnp.int32)
    hits = target[:, None, :] == r[None, :, None]

    def pack(place, count):
        return (place.reshape(1, -1) == jnp.arange(count, dtype=jnp.int32)[:, None]).astype(jnp.bfloat16)

    def unpack(place, count):
        there = jnp.max(jnp.where(hits, place[:, None, :], -1), axis=2).reshape(-1, 1)
        return (there == jnp.arange(count, dtype=jnp.int32)[None, :]).astype(jnp.bfloat16)

    places = [positions(far == f) for f in (0, 2, 3)]
    packs = [pack(p, c) for p, c in zip(places, caps)]
    unpacks = [unpack(jnp.where(far == f, flat, -1), slices * rows) for f in (1, 0)]
    unpacks += [unpack(p, c) for p, c in zip(places, caps)]
    return packs, unpacks


def render_kernel(
    slices, rows, last_lat, front_ref, shift_ref, par_ref, own_m, top_m, up_m, one_m, two_m, own, up, one, two, out_ref, cells
):
    lobes = par_ref.shape[1]
    tile = 256
    lat = lax.axis_index("lat")

    def classify(samples):
        sums = None
        for k in range(lobes):
            off = samples - par_ref[0, k]
            lobe = jnp.exp2(off * off * par_ref[1, k])
            terms = [par_ref[2 + j, k] * lobe for j in range(4)]
            sums = terms if sums is None else [a + b for a, b in zip(sums, terms)]
        return tuple(sums)

    def fill(pairs):
        @pl.loop(0, cells.shape[0], step=tile)
        def _(start):
            at = pl.ds(pl.multiple_of(start, tile), tile)
            total = None
            for m, rows_ref in pairs:
                term = jnp.dot(m[at, :], rows_ref[...], preferred_element_type=jnp.float32)
                total = term if total is None else total + term
            cells[at, :] = total

    def cast(band, limit):
        forward = front_ref[0, band] == 0
        for part in range(out_ref.shape[3] // LANES):
            lanes = slice(part * LANES, (part + 1) * LANES)
            zero = jnp.zeros((rows, LANES), jnp.float32)
            empty = None if limit is None else classify(zero)

            def advance(i, carry):
                depth, clear, red, green, blue = carry
                z = jnp.where(forward, i, slices - 1 - i)

                def filled():
                    return classify(cells[pl.ds(pl.multiple_of(z * rows, rows), rows), lanes])

                if limit is None:
                    sums = filled()
                else:
                    sums = lax.cond(shift_ref[0, z] >= limit, lambda: empty, filled)
                depth = depth + sums[0]
                after = jnp.exp2(-depth)
                weight = clear - after
                return (depth, after, red + weight * sums[1], green + weight * sums[2], blue + weight * sums[3])

            depth, _, red, green, blue = lax.fori_loop(
                0, slices, advance, (zero, zero + 1.0, zero, zero, zero), unroll=2 if limit is None else 1
            )
            out_ref[band, 0, :, lanes] = red
            out_ref[band, 1, :, lanes] = green
            out_ref[band, 2, :, lanes] = blue
            out_ref[band, 3, :, lanes] = depth

    fill([(own_m, own), (up_m, up), (one_m, one), (two_m, two)])

    @pl.when(lat != last_lat)
    def _():
        cast(0, None)
        out_ref[1] = jnp.zeros(out_ref.shape[1:], jnp.float32)

    @pl.when(lat == last_lat)
    def _():
        cast(0, 2 * rows)
        fill([(top_m, own)])
        cast(1, rows)


def render(front, shift, params, unpacks, field, up, one, two, chunk, slabs):
    slices = shift.shape[1]
    total, cols = field.shape
    rows = total // slices
    block = cols // slabs // CHUNKS
    stride = cols // slabs // block

    def whole(m):
        return pl.BlockSpec(m.shape, lambda c: (0, 0))

    def columns(a):
        return pl.BlockSpec((a.shape[0], block), lambda c: (0, c))

    smem = pl.BlockSpec(memory_space=pltpu.SMEM)
    cells = total * block * slabs
    last = lax.axis_size("lat") - 1
    return pl.pallas_call(
        lambda *refs: render_kernel(slices, rows, last, *refs),
        out_shape=jax.ShapeDtypeStruct((2, 4, rows, block * slabs), jnp.float32),
        grid=(slabs,),
        in_specs=[smem] * 3
        + [whole(m) for m in unpacks]
        + [pl.BlockSpec((total, block), lambda c: (0, c * stride + chunk))]
        + [columns(a) for a in (up, one, two)],
        out_specs=pl.BlockSpec((2, 4, rows, block), lambda c: (0, 0, 0, c)),
        scratch_shapes=[pltpu.VMEM((total, block), jnp.float32)],
        compiler_params=pltpu.CompilerParams(vmem_limit_bytes=48 * 1024 * 1024),
        cost_estimate=pl.CostEstimate(flops=cells * 24000, bytes_accessed=cells * 6, transcendentals=cells * 9),
        name="render",
    )(front, shift, params, *unpacks, field, up, one, two)


def pick(matrix, rows):
    return jnp.dot(matrix, rows, preferred_element_type=jnp.float32).astype(jnp.bfloat16)


def images(packs, unpacks, field, shift, orders, params):
    slabs = lax.axis_size("depth")
    slab = lax.axis_index("depth")
    last = lax.axis_index("lat") == lax.axis_size("lat") - 1
    total, cols = field.shape
    width = cols // slabs // CHUNKS
    front = orders[:, :1].T
    arrived = []
    for c in range(CHUNKS):
        own = jnp.concatenate(
            [field[:, s * (cols // slabs) + c * width :][:, :width] for s in range(slabs)], axis=1
        )
        arrived.append([along_lat(pick(m, own), d) for m, d in zip(packs, (1, -1, -2))])
    out = []
    mine_first = (orders[:, 0] == slab)[:, None, None, None]
    for c in range(CHUNKS):
        part = render(front, shift[None], params, unpacks, field, *arrived[c], c, slabs)
        theirs = lax.dynamic_slice_in_dim(part, (1 - slab) * width, width, 3)
        mine = lax.dynamic_slice_in_dim(part, slab * width, width, 3)
        other = lax.ppermute(theirs, "depth", [(0, 1), (1, 0)])
        near = jnp.where(mine_first, mine, other)
        behind = jnp.where(mine_first, other, mine)
        color = near[:, :3] + jnp.exp2(-near[:, 3:]) * behind[:, :3]
        opacity = 1.0 - jnp.exp2(-(mine[:, 3:] + other[:, 3:]))
        bands = jnp.concatenate([color, opacity], axis=1)
        out.append(jnp.where(last, bands[1], along_lat(bands[0], -1)))
    return jnp.concatenate(out, axis=2)


def local(volume, shift_table, slab_order, centers, widths, extinct, colors):
    slabs = lax.axis_size("depth")
    slices, rows, cols = volume.shape
    total = slices * rows
    log2e = math.log2(math.e)
    inv_depth = log2e / (slices * slabs)
    params = jnp.concatenate(
        [centers[None], (widths * -log2e)[None], (extinct * inv_depth)[None], colors], axis=0
    )
    slab = lax.axis_index("depth")
    shift = lax.dynamic_slice_in_dim(shift_table, slab * slices, slices)
    orders = jnp.concatenate([along_lat(slab_order, 1), slab_order], axis=0)
    caps = (total * 5 // 16, total * 15 // 32, total * 5 // 16)
    full = (total,) * 3
    over = jnp.zeros((), jnp.int32)
    _, all_far = plan(shift_table, rows)
    for s in range(slabs):
        far = all_far[s * slices : (s + 1) * slices]
        for f, cap in zip((0, 2, 3), caps):
            over = jnp.maximum(over, jnp.sum((far == f).astype(jnp.int32)) - cap)
    over = max_over(over.reshape(1, 1), "views")[0, 0]
    packs, unpacks = tables(shift, rows, caps)
    field = volume.reshape(total, cols)
    return lax.cond(
        over > 0,
        lambda p, u, f, s, *a: images(*tables(s, rows, full), f, s, *a),
        images,
        packs,
        unpacks,
        field,
        shift,
        orders,
        params,
    )


def solution(mesh):
    in_specs = (
        P(("views", "depth"), "lat", None),
        P("views"),
        P(("views", "lat"), None),
        P(),
        P(),
        P(),
        P(),
    )
    out_specs = P(None, ("views", "lat"), "depth")
    return jax.shard_map(local, mesh=mesh, in_specs=in_specs, out_specs=out_specs, check_vma=False)
```

```python
import math
import jax
import jax.numpy as jnp
from jax import lax
from jax.experimental import pallas as pl
from jax.experimental.pallas import tpu as pltpu
from jax.sharding import PartitionSpec as P

CHUNKS = 2
BLOCK = 256


def along_lat(block, distance):
    devices = range(lax.axis_size("lat"))
    route = [(i, i + distance) for i in devices if i + distance in devices]
    return lax.ppermute(block, "lat", route)


def max_over(value, axis):
    size = lax.axis_size(axis)
    best = value
    for step in range(1, size):
        route = [(i, (i + step) % size) for i in range(size)]
        best = jnp.maximum(best, lax.ppermute(value, axis, route))
    return best


def positions(wanted):
    slices, rows = wanted.shape
    ones = wanted.astype(jnp.int32)
    z = jnp.arange(slices, dtype=jnp.int32)
    counts = jnp.sum(ones, axis=1)
    base = jnp.sum(jnp.where(z[None, :] < z[:, None], counts[None, :], 0), axis=1)
    r = jnp.arange(rows, dtype=jnp.int32)
    rank = jnp.sum(jnp.where(r[None, :, None] > r[None, None, :], ones[:, None, :], 0), axis=2)
    return jnp.where(wanted, base[:, None] + rank, -1)


def plan(shift, rows):
    source = jnp.arange(rows, dtype=jnp.int32)[None, :]
    target = (source - shift[:, None]) % rows
    far = (target + shift[:, None]) // rows
    return target, far


def tables(shift, rows, caps):
    slices = shift.shape[0]
    target, far = plan(shift, rows)
    flat = jnp.arange(slices * rows, dtype=jnp.int32).reshape(slices, rows)
    r = jnp.arange(rows, dtype=jnp.int32)
    hits = target[:, None, :] == r[None, :, None]

    def pack(place, count):
        return (place.reshape(1, -1) == jnp.arange(count, dtype=jnp.int32)[:, None]).astype(jnp.bfloat16)

    def unpack(place, count):
        there = jnp.max(jnp.where(hits, place[:, None, :], -1), axis=2).reshape(-1, 1)
        return (there == jnp.arange(count, dtype=jnp.int32)[None, :]).astype(jnp.bfloat16)

    places = [positions(far == f) for f in (0, 2, 3)]
    packs = [pack(p, c) for p, c in zip(places, caps)]
    unpacks = [unpack(jnp.where(far == f, flat, -1), slices * rows) for f in (1, 0)]
    unpacks += [unpack(p, c) for p, c in zip(places, caps)]
    return packs, unpacks


def render_kernel(
    slices, rows, last_lat, front_ref, shift_ref, par_ref, own_m, top_m, up_m, one_m, two_m, own, up, one, two, out_ref, cells
):
    lobes = par_ref.shape[1]
    tile = 256
    lat = lax.axis_index("lat")

    def classify(samples):
        sums = None
        for k in range(lobes):
            off = samples - par_ref[0, k]
            lobe = jnp.exp2(off * off * par_ref[1, k])
            terms = [par_ref[2 + j, k] * lobe for j in range(4)]
            sums = terms if sums is None else [a + b for a, b in zip(sums, terms)]
        return tuple(sums)

    def fill(pairs):
        @pl.loop(0, cells.shape[0], step=tile)
        def _(start):
            at = pl.ds(pl.multiple_of(start, tile), tile)
            total = None
            for m, rows_ref in pairs:
                term = jnp.dot(m[at, :], rows_ref[...], preferred_element_type=jnp.float32)
                total = term if total is None else total + term
            cells[at, :] = total

    def cast(band, limit):
        forward = front_ref[0, band] == 0
        zero = jnp.zeros((rows, out_ref.shape[3]), jnp.float32)
        empty = None if limit is None else classify(zero)

        def advance(i, carry):
            depth, clear, red, green, blue = carry
            z = jnp.where(forward, i, slices - 1 - i)

            def filled():
                return classify(cells[pl.ds(pl.multiple_of(z * rows, rows), rows), :])

            if limit is None:
                sums = filled()
            else:
                sums = lax.cond(shift_ref[0, z] >= limit, lambda: empty, filled)
            depth = depth + sums[0]
            after = jnp.exp2(-depth)
            weight = clear - after
            return (depth, after, red + weight * sums[1], green + weight * sums[2], blue + weight * sums[3])

        depth, _, red, green, blue = lax.fori_loop(
            0, slices, advance, (zero, zero + 1.0, zero, zero, zero), unroll=2 if limit is None else 1
        )
        out_ref[band, 0] = red
        out_ref[band, 1] = green
        out_ref[band, 2] = blue
        out_ref[band, 3] = depth

    fill([(own_m, own), (up_m, up), (one_m, one), (two_m, two)])

    @pl.when(lat != last_lat)
    def _():
        cast(0, None)
        out_ref[1] = jnp.zeros(out_ref.shape[1:], jnp.float32)

    @pl.when(lat == last_lat)
    def _():
        cast(0, 2 * rows)
        fill([(top_m, own)])
        cast(1, rows)


def render(front, shift, params, unpacks, field, up, one, two, chunk, slabs):
    slices = shift.shape[1]
    total, cols = field.shape
    rows = total // slices
    width = cols // slabs // CHUNKS
    block = min(BLOCK, width)
    stride = cols // slabs // block
    steps = width // block

    def whole(m):
        return pl.BlockSpec(m.shape, lambda c: (0, 0))

    def columns(a):
        return pl.BlockSpec((a.shape[0], block), lambda c: (0, c))

    smem = pl.BlockSpec(memory_space=pltpu.SMEM)
    cells = total * width * slabs
    last = lax.axis_size("lat") - 1
    return pl.pallas_call(
        lambda *refs: render_kernel(slices, rows, last, *refs),
        out_shape=jax.ShapeDtypeStruct((2, 4, rows, width * slabs), jnp.float32),
        grid=(slabs * steps,),
        in_specs=[smem] * 3
        + [whole(m) for m in unpacks]
        + [pl.BlockSpec((total, block), lambda c: (0, c // steps * stride + chunk * steps + c % steps))]
        + [columns(a) for a in (up, one, two)],
        out_specs=pl.BlockSpec((2, 4, rows, block), lambda c: (0, 0, 0, c)),
        scratch_shapes=[pltpu.VMEM((total, block), jnp.float32)],
        compiler_params=pltpu.CompilerParams(vmem_limit_bytes=48 * 1024 * 1024),
        cost_estimate=pl.CostEstimate(flops=cells * 24000, bytes_accessed=cells * 6, transcendentals=cells * 9),
        name="render",
    )(front, shift, params, *unpacks, field, up, one, two)


def pick(matrix, rows):
    return jnp.dot(matrix, rows, preferred_element_type=jnp.float32).astype(jnp.bfloat16)


def images(packs, unpacks, field, shift, orders, params):
    slabs = lax.axis_size("depth")
    slab = lax.axis_index("depth")
    last = lax.axis_index("lat") == lax.axis_size("lat") - 1
    total, cols = field.shape
    width = cols // slabs // CHUNKS
    front = orders[:, :1].T
    arrived = []
    for c in range(CHUNKS):
        own = jnp.concatenate(
            [field[:, s * (cols // slabs) + c * width :][:, :width] for s in range(slabs)], axis=1
        )
        arrived.append([along_lat(pick(m, own), d) for m, d in zip(packs, (1, -1, -2))])
    out = []
    mine_first = (orders[:, 0] == slab)[:, None, None, None]
    for c in range(CHUNKS):
        part = render(front, shift[None], params, unpacks, field, *arrived[c], c, slabs)
        theirs = lax.dynamic_slice_in_dim(part, (1 - slab) * width, width, 3)
        mine = lax.dynamic_slice_in_dim(part, slab * width, width, 3)
        other = lax.ppermute(theirs, "depth", [(0, 1), (1, 0)])
        near = jnp.where(mine_first, mine, other)
        behind = jnp.where(mine_first, other, mine)
        color = near[:, :3] + jnp.exp2(-near[:, 3:]) * behind[:, :3]
        opacity = 1.0 - jnp.exp2(-(mine[:, 3:] + other[:, 3:]))
        bands = jnp.concatenate([color, opacity], axis=1)
        out.append(jnp.where(last, bands[1], along_lat(bands[0], -1)))
    return jnp.concatenate(out, axis=2)


def local(volume, shift_table, slab_order, centers, widths, extinct, colors):
    slabs = lax.axis_size("depth")
    slices, rows, cols = volume.shape
    total = slices * rows
    log2e = math.log2(math.e)
    inv_depth = log2e / (slices * slabs)
    params = jnp.concatenate(
        [centers[None], (widths * -log2e)[None], (extinct * inv_depth)[None], colors], axis=0
    )
    slab = lax.axis_index("depth")
    shift = lax.dynamic_slice_in_dim(shift_table, slab * slices, slices)
    orders = jnp.concatenate([along_lat(slab_order, 1), slab_order], axis=0)
    caps = (total * 5 // 16, total * 15 // 32, total * 5 // 16)
    full = (total,) * 3
    over = jnp.zeros((), jnp.int32)
    _, all_far = plan(shift_table, rows)
    for s in range(slabs):
        far = all_far[s * slices : (s + 1) * slices]
        for f, cap in zip((0, 2, 3), caps):
            over = jnp.maximum(over, jnp.sum((far == f).astype(jnp.int32)) - cap)
    over = max_over(over.reshape(1, 1), "views")[0, 0]
    packs, unpacks = tables(shift, rows, caps)
    field = volume.reshape(total, cols)
    return lax.cond(
        over > 0,
        lambda p, u, f, s, *a: images(*tables(s, rows, full), f, s, *a),
        images,
        packs,
        unpacks,
        field,
        shift,
        orders,
        params,
    )


def solution(mesh):
    in_specs = (
        P(("views", "depth"), "lat", None),
        P("views"),
        P(("views", "lat"), None),
        P(),
        P(),
        P(),
        P(),
    )
    out_specs = P(None, ("views", "lat"), "depth")
    return jax.shard_map(local, mesh=mesh, in_specs=in_specs, out_specs=out_specs, check_vma=False)
```

```python
import math
import jax
import jax.numpy as jnp
from jax import lax
from jax.experimental import pallas as pl
from jax.experimental.pallas import tpu as pltpu
from jax.sharding import PartitionSpec as P

CHUNKS = 4
BLOCK = 256
TILE = 256


def from_behind(block, axis, distance):
    devices = range(lax.axis_size(axis))
    route = [(i - distance, i) for i in devices if i - distance in devices]
    return lax.ppermute(block, axis, route)


def max_over(value, axis):
    size = lax.axis_size(axis)
    best = value
    for step in range(1, size):
        route = [(i, (i + step) % size) for i in range(size)]
        best = jnp.maximum(best, lax.ppermute(value, axis, route))
    return best


def exclusive(counts):
    z = jnp.arange(counts.shape[0], dtype=jnp.int32)
    return jnp.sum(jnp.where(z[None, :] < z[:, None], counts[None, :], 0), axis=1)


def positions(wanted):
    slices, rows = wanted.shape
    ones = wanted.astype(jnp.int32)
    base = exclusive(jnp.sum(ones, axis=1))
    r = jnp.arange(rows, dtype=jnp.int32)
    rank = jnp.sum(jnp.where(r[None, :, None] > r[None, None, :], ones[:, None, :], 0), axis=2)
    return jnp.where(wanted, base[:, None] + rank, -1)


def plan(local_shift, rows):
    source = jnp.arange(rows, dtype=jnp.int32)[None, :]
    target = (source - local_shift[:, None]) % rows
    far = (target + local_shift[:, None]) // rows
    return target, far


def one_hot(place, count):
    return (place.reshape(1, -1) == jnp.arange(count, dtype=jnp.int32)[:, None]).astype(jnp.bfloat16)


def render_kernel(slices, rows, front_ref, par_ref, own_m, two_m, odd_m, own, two, odd, out_ref, cells):
    lobes = par_ref.shape[1]
    tile = own_m.shape[1]

    @pl.loop(0, cells.shape[0], step=tile)
    def _(start):
        at = pl.ds(pl.multiple_of(start, tile), tile)
        cells[at, :] = (
            jnp.dot(own_m[at, :], own[at, :], preferred_element_type=jnp.float32)
            + jnp.dot(two_m[at, :], two[...], preferred_element_type=jnp.float32)
            + jnp.dot(odd_m[at, :], odd[...], preferred_element_type=jnp.float32)
        )

    forward = front_ref[0, 0] == 0

    def advance(i, carry):
        depth, clear, red, green, blue = carry
        z = jnp.where(forward, i, slices - 1 - i)
        samples = cells[pl.ds(pl.multiple_of(z * rows, rows), rows), :]
        sums = None
        for k in range(lobes):
            off = samples - par_ref[0, k]
            lobe = jnp.exp2(off * off * par_ref[1, k])
            terms = [par_ref[2 + j, k] * lobe for j in range(4)]
            sums = terms if sums is None else [a + b for a, b in zip(sums, terms)]
        depth = depth + sums[0]
        after = jnp.exp2(-depth)
        weight = clear - after
        return (depth, after, red + weight * sums[1], green + weight * sums[2], blue + weight * sums[3])

    zero = jnp.zeros(out_ref.shape[1:], jnp.float32)
    depth, _, red, green, blue = lax.fori_loop(0, slices, advance, (zero, zero + 1.0, zero, zero, zero), unroll=2)
    out_ref[0] = red
    out_ref[1] = green
    out_ref[2] = blue
    out_ref[3] = depth


def render(front, params, matrices, own, two, odd, slices, rows):
    cols = own.shape[1]
    block = min(BLOCK, cols)

    def whole(m):
        return pl.BlockSpec(m.shape, lambda c: (0, 0))

    def columns(a):
        return pl.BlockSpec((a.shape[0], block), lambda c: (0, c))

    smem = pl.BlockSpec(memory_space=pltpu.SMEM)
    cells = slices * rows * cols
    return pl.pallas_call(
        lambda *refs: render_kernel(slices, rows, *refs),
        out_shape=jax.ShapeDtypeStruct((4, rows, cols), jnp.float32),
        grid=(cols // block,),
        in_specs=[smem, smem] + [whole(m) for m in matrices] + [columns(a) for a in (own, two, odd)],
        out_specs=pl.BlockSpec((4, rows, block), lambda c: (0, 0, c)),
        scratch_shapes=[pltpu.VMEM((slices * rows, block), jnp.float32)],
        compiler_params=pltpu.CompilerParams(vmem_limit_bytes=40 * 1024 * 1024),
        cost_estimate=pl.CostEstimate(flops=cells * 24000, bytes_accessed=cells * 6, transcendentals=cells * 9),
        name="render",
    )(front, params, *matrices, own, two, odd)


def pick(matrix, rows):
    return jnp.dot(matrix, rows, preferred_element_type=jnp.float32).astype(jnp.bfloat16)


def partial_image(two_cap, odd_cap, volume, local_shift, front, params):
    slices, rows, cols = volume.shape
    total = slices * rows
    target, far = plan(local_shift, rows)
    two_at = positions(far >= 2)
    odd_at = positions(far % 2 == 1)
    two_send = one_hot(two_at, two_cap)
    odd_own = one_hot(jnp.where(far == 1, odd_at, -1), odd_cap)
    two_index = jnp.arange(two_cap, dtype=jnp.int32)
    hop = jnp.where(far == 3, two_at, -1).reshape(1, -1)
    odd_two = jnp.dot(
        one_hot(odd_at, odd_cap),
        (hop.reshape(-1, 1) == two_index[None, :]).astype(jnp.bfloat16),
        preferred_element_type=jnp.float32,
    ).astype(jnp.bfloat16)
    source = jnp.arange(rows, dtype=jnp.int32)
    picks = target[:, None, :] == source[None, :, None]

    def by_target(values):
        return jnp.max(jnp.where(picks, values[:, None, :], -1), axis=2).reshape(-1, 1)

    tile = math.gcd(total, max(TILE, rows))
    flat = jnp.arange(total, dtype=jnp.int32).reshape(slices, rows)

    def place(values, count):
        return (by_target(values) == jnp.arange(count, dtype=jnp.int32)[None, :]).astype(jnp.bfloat16)

    matrices = (
        place(jnp.where(far == 0, flat % tile, -1), tile),
        place(jnp.where(far == 2, two_at, -1), two_cap),
        place(odd_at, odd_cap),
    )
    field = volume.reshape(total, cols)
    width = cols // CHUNKS
    parts = []
    owns = [field[:, c * width : (c + 1) * width] for c in range(CHUNKS)]
    twos = []
    for c in range(CHUNKS):
        if c >= 2:
            owns[c], twos[c - 2] = lax.optimization_barrier((owns[c], twos[c - 2]))
        twos.append(from_behind(pick(two_send, owns[c]), "lat", -2))
    for c, (own, two) in enumerate(zip(owns, twos)):
        if c >= 2:
            two, parts[c - 2] = lax.optimization_barrier((two, parts[c - 2]))
        relay = jnp.dot(odd_own, own, preferred_element_type=jnp.float32) + jnp.dot(
            odd_two, two, preferred_element_type=jnp.float32
        )
        odd = from_behind(relay.astype(jnp.bfloat16), "lat", -1)
        parts.append(render(front, params, matrices, own, two, odd, slices, rows))
    return jnp.concatenate(parts, axis=2)


def local(volume, shift_table, slab_order, centers, widths, extinct, colors):
    slabs = lax.axis_size("depth")
    slices, rows, cols = volume.shape
    total = slices * rows
    log2e = math.log2(math.e)
    inv_depth = log2e / (slices * slabs)
    params = jnp.concatenate(
        [centers[None], (widths * -log2e)[None], (extinct * inv_depth)[None], colors], axis=0
    )
    slab = lax.axis_index("depth")
    local_shift = lax.dynamic_slice_in_dim(shift_table, slab * slices, slices)
    two_cap, odd_cap = total * 11 // 16, total * 10 // 16
    over = jnp.zeros((), jnp.int32)
    _, all_far = plan(shift_table, rows)
    for s in range(slabs):
        far = all_far[s * slices : (s + 1) * slices]
        over = jnp.maximum(over, jnp.sum((far >= 2).astype(jnp.int32)) - two_cap)
        over = jnp.maximum(over, jnp.sum((far % 2 == 1).astype(jnp.int32)) - odd_cap)
    over = max_over(over.reshape(1, 1), "views")[0, 0]
    partial_value = lax.cond(
        over > 0,
        lambda *a: partial_image(total, total, *a),
        lambda *a: partial_image(two_cap, odd_cap, *a),
        volume,
        local_shift,
        slab_order,
        params,
    )
    own_cols = cols // slabs
    theirs = lax.dynamic_slice_in_dim(partial_value, (1 - slab) * own_cols, own_cols, 2)
    mine = lax.dynamic_slice_in_dim(partial_value, slab * own_cols, own_cols, 2)
    other = lax.ppermute(theirs, "depth", [(0, 1), (1, 0)])
    mine_first = slab_order[0, 0] == slab
    front = jnp.where(mine_first, mine, other)
    back = jnp.where(mine_first, other, mine)
    color = front[:3] + jnp.exp2(-front[3])[None] * back[:3]
    opacity = 1.0 - jnp.exp2(-(mine[3] + other[3]))
    return jnp.concatenate([color, opacity[None]], axis=0)


def solution(mesh):
    in_specs = (
        P(("views", "depth"), "lat", None),
        P("views"),
        P(("views", "lat"), None),
        P(),
        P(),
        P(),
        P(),
    )
    out_specs = P(None, ("views", "lat"), "depth")
    return jax.shard_map(local, mesh=mesh, in_specs=in_specs, out_specs=out_specs, check_vma=False)
```
